32 devices in a mesh: lon: 2 (over core), lat: 16 (over z, y, x).
Axes of the slice: x: 2, y: 2, z: 4, core: 2. Of those that a mesh axis runs over, the one named last changes fastest.
Arguments:
- ocean_state: bfloat16 [1, 96, 128, 256], P(None, 'lat', 'lon'), may hold values from -6 to 6
- land_sea: int32 [1, 96, 128], P(None, 'lat', 'lon'), may hold values 0 or 1
- cotangent: bfloat16 [1, 96, 128, 256], P(None, 'lat', 'lon'), may hold values from -6 to 6
- dw_kernel: float32 [7, 7, 256], replicated, may hold values from -0.875 to 0.875
- dw_bias: float32 [256], replicated, may hold values from -3 to 3
- ln_gain: float32 [256], replicated, may hold values from 0.1 to 1.9
- ln_bias: float32 [256], replicated, may hold values from -2 to 2
- w_in: bfloat16 [256, 1024], replicated, may hold values from -0.375 to 0.375
- b_in: float32 [1024], replicated, may hold values from -2 to 2
- w_out: bfloat16 [1024, 256], replicated, may hold values from -0.1875 to 0.1875
- b_out: float32 [256], replicated, may hold values from -2 to 2
- layer_scale: float32 [256], replicated, may hold values from 0.3 to 1.5
Outputs:
- output: bfloat16 [1, 96, 128, 256], P(None, 'lat', 'lon')
- grad_state: bfloat16 [1, 96, 128, 256], P(None, 'lat', 'lon')
- grad_kernel: float32 [7, 7, 256], replicated
- grad_dw_bias: float32 [256], replicated
- grad_ln_gain: float32 [256], replicated
- grad_ln_bias: float32 [256], replicated
- grad_w_in: float32 [256, 1024], replicated
- grad_b_in: float32 [1024], replicated
- grad_w_out: float32 [1024, 256], replicated
- grad_b_out: float32 [256], replicated
- grad_scale: float32 [256], replicated
The draws below stay inside these ranges and needn't reach their ends.
All inputs are finite; a program needn't handle non-finite values. No bound on the sum of `land_sea` on one device may be relied on, other than what follows from the above.
Results may differ from the reference program's by a relative error of at most 0.0085.
Values may be sent and summed in bfloat16 or wider, within the bound.
A program may use at most 64 MiB of HBM per device.

```python
import math
import jax
import jax.numpy as jnp
from jax import lax

C = 256
HID = 1024
BATCH = 1
LAT = 96
LON = 128


def place_ends(result, stream_key, smallest, high):
    shape = result.shape
    place = [jax.random.randint(jax.random.fold_in(stream_key, axis), (), 0, shape[axis]) for axis in range(len(shape))]
    result = result.at[tuple(place)].set(smallest)
    longest = shape.index(max(shape))
    place[longest] = (place[longest] + 1) % shape[longest]
    return result.at[tuple(place)].set(high)


def levels(own_key, shape, split, low, top_value):
    factor_of = 1.0
    for dim, shards_of in split:
        steps = jax.random.uniform(jax.random.fold_in(jax.random.fold_in(own_key, 6), dim), (shards_of,), jnp.float32, low / len(split), top_value / len(split))
        factor_of = factor_of * jnp.repeat(jnp.exp(steps), shape[dim] // shards_of).reshape((-1,) + (1,) * (len(shape) - 1 - dim))
    return factor_of


def bell_draw(key, shape, deviation, limit, shards=(), dtype=jnp.bfloat16):
    drawn = jax.random.normal(key, shape, jnp.float32) * deviation
    if len(shards) > 0:
        drawn = levels(key, shape, shards, -0.22, 0.18) * drawn
    return jnp.clip(drawn, min=-limit, max=limit).astype(dtype)


def setup_inputs(seed: int = 0) -> dict:
    splits = jax.random.split(jax.random.key(seed), 13)
    ocean_state = bell_draw(splits[0], (BATCH, LAT, LON, C), 1.0, 6.0, ((1, 16), (2, 2)))
    land_sea = place_ends((jax.random.randint(splits[1], (BATCH, LAT, LON), 0, 3) < 2).astype(jnp.int32), jax.random.fold_in(splits[1], 1), 0, 1)
    cotangent = bell_draw(splits[2], (BATCH, LAT, LON, C), 1.0, 6.0, ((1, 16), (2, 2)))
    dw_kernel = bell_draw(splits[3], (7, 7, C), 49 ** -0.5, 0.875, (), jnp.float32)
    dw_bias = bell_draw(splits[4], (C,), 0.5, 3.0, (), jnp.float32)
    ln_gain = jnp.clip(1.0 + 0.18 * jax.random.normal(splits[5], (C,), jnp.float32), 0.1, 1.9)
    ln_bias = bell_draw(splits[6], (C,), 0.3, 2.0, (), jnp.float32)
    w_in = bell_draw(splits[7], (C, HID), C ** -0.5, 0.375)
    b_in = bell_draw(splits[8], (HID,), 0.3, 2.0, (), jnp.float32)
    w_out = bell_draw(splits[9], (HID, C), HID ** -0.5, 0.1875)
    b_out = bell_draw(splits[10], (C,), 0.3, 2.0, (), jnp.float32)
    layer_scale = jnp.clip(jnp.exp(jax.random.uniform(splits[11], (C,), jnp.float32, math.log(0.3), math.log(1.5))), 0.3, 1.5)
    return {"ocean_state": ocean_state, "land_sea": land_sea, "cotangent": cotangent, "dw_kernel": dw_kernel, "dw_bias": dw_bias, "ln_gain": ln_gain, "ln_bias": ln_bias, "w_in": w_in, "b_in": b_in, "w_out": w_out, "b_out": b_out, "layer_scale": layer_scale}


def depthwise(padded, kernel, num_rows, num_cols):
    summed = jnp.zeros((padded.shape[0], num_rows, num_cols, padded.shape[3]), jnp.float32)
    for row_off in range(7):
        for col_off in range(7):
            summed = summed + padded[:, row_off:row_off + num_rows, col_off:col_off + num_cols, :].astype(jnp.float32) * kernel[row_off, col_off]
    return summed

def transposed(padded, kernel, num_rows, num_cols):
    summed = jnp.zeros((padded.shape[0], num_rows, num_cols, padded.shape[3]), jnp.float32)
    for row_off in range(7):
        for col_off in range(7):
            summed = summed + padded[:, 6 - row_off:6 - row_off + num_rows, 6 - col_off:6 - col_off + num_cols, :].astype(jnp.float32) * kernel[row_off, col_off]
    return summed

def kernel_terms(padded, grad_depth, num_rows, num_cols):
    grad_float = grad_depth.astype(jnp.float32)
    rows_out = []
    for row_off in range(7):
        cols_out = []
        for col_off in range(7):
            window = padded[:, row_off:row_off + num_rows, col_off:col_off + num_cols, :].astype(jnp.float32)
            cols_out.append(lax.optimization_barrier(jnp.sum(window * grad_float, axis=(0, 1, 2))))
        rows_out.append(jnp.stack(cols_out))
    return jnp.stack(rows_out)

def forward_tokens(depth_out, ln_gain, ln_bias, w_in, b_in, w_out, b_out):
    center = depth_out - lax.optimization_barrier(jnp.mean(depth_out, axis=-1, keepdims=True))
    inv_std = lax.rsqrt(lax.optimization_barrier(jnp.mean(center * center, axis=-1, keepdims=True)) + 1e-06)
    norm_hat = center * inv_std
    normed = (norm_hat * ln_gain + ln_bias).astype(jnp.bfloat16)
    pre_act = jnp.dot(normed, w_in, preferred_element_type=jnp.float32) + b_in
    activated = jax.nn.gelu(pre_act, approximate=True).astype(jnp.bfloat16)
    branch = jnp.dot(activated, w_out, preferred_element_type=jnp.float32) + b_out
    return (norm_hat, inv_std, normed, pre_act, activated, branch)

def backward_tokens(masked, norm_hat, inv_std, pre_act, ln_gain, w_in, w_out, layer_scale):
    grad_branch = (masked * layer_scale).astype(jnp.bfloat16)
    grad_act = lax.dot_general(grad_branch, w_out, (((1,), (1,)), ((), ())), preferred_element_type=jnp.float32)
    unused, pull_back = jax.vjp(lambda v: jax.nn.gelu(v, approximate=True), pre_act)
    grad_pre = pull_back(grad_act)[0].astype(jnp.bfloat16)
    grad_norm = lax.dot_general(grad_pre, w_in, (((1,), (1,)), ((), ())), preferred_element_type=jnp.float32)
    scaled = grad_norm * ln_gain
    grad_depth = (inv_std * (scaled - lax.optimization_barrier(jnp.mean(scaled, axis=-1, keepdims=True)) - norm_hat * lax.optimization_barrier(jnp.mean(scaled * norm_hat, axis=-1, keepdims=True)))).astype(jnp.bfloat16)
    return (grad_branch, grad_pre, grad_norm, grad_depth)

def weight_terms(masked, branch, grad_branch, activated, normed, grad_pre, grad_norm, norm_hat):
    dims = (((0,), (0,)), ((), ()))
    grad_w_in = lax.dot_general(normed, grad_pre, dims, preferred_element_type=jnp.float32)
    grad_w_out = lax.dot_general(activated, grad_branch, dims, preferred_element_type=jnp.float32)
    return (grad_w_in, grad_w_out, lax.optimization_barrier(jnp.sum(grad_pre.astype(jnp.float32), axis=0)), lax.optimization_barrier(jnp.sum(grad_branch.astype(jnp.float32), axis=0)), lax.optimization_barrier(jnp.sum(masked * branch, axis=0)), lax.optimization_barrier(jnp.sum(grad_norm * norm_hat, axis=0)), lax.optimization_barrier(jnp.sum(grad_norm, axis=0)))

def rim_pad(field):
    lon_ext = jnp.concatenate([field[:, :, -3:], field, field[:, :, :3]], axis=2)
    return jnp.pad(lon_ext, ((0, 0), (3, 3), (0, 0), (0, 0)))

def reference(ocean_state, land_sea, cotangent, dw_kernel, dw_bias, ln_gain, ln_bias, w_in, b_in, w_out, b_out, layer_scale):
    num_batch, num_rows, num_cols, channels = ocean_state.shape
    padded = rim_pad(ocean_state)
    depth_out = depthwise(padded, dw_kernel, num_rows, num_cols) + dw_bias
    mask_float = land_sea.astype(jnp.float32)[..., None]
    masked = mask_float * cotangent.astype(jnp.float32)
    depth_rows = depth_out.reshape(num_batch * num_rows, num_cols, channels)
    masked_rows = masked.reshape(num_batch * num_rows, num_cols, channels)
    hidden = w_in.shape[1]
    start = (jnp.zeros((channels, hidden), jnp.float32), jnp.zeros((hidden, channels), jnp.float32), jnp.zeros((hidden,), jnp.float32), jnp.zeros((channels,), jnp.float32), jnp.zeros((channels,), jnp.float32), jnp.zeros((channels,), jnp.float32), jnp.zeros((channels,), jnp.float32))

    def one_row(running, pieces):
        depth_row, masked_row = pieces
        norm_hat, inv_std, normed, pre_act, activated, branch = forward_tokens(depth_row, ln_gain, ln_bias, w_in, b_in, w_out, b_out)
        grad_branch, grad_pre, grad_norm, grad_depth = backward_tokens(masked_row, norm_hat, inv_std, pre_act, ln_gain, w_in, w_out, layer_scale)
        fresh = weight_terms(masked_row, branch, grad_branch, activated, normed, grad_pre, grad_norm, norm_hat)
        return (jax.tree.map(lambda a, b: a + b, running, fresh), (branch, grad_depth))
    totals, (branch_rows, grad_rows) = lax.scan(one_row, start, (depth_rows, masked_rows))
    branch = branch_rows.reshape(num_batch, num_rows, num_cols, channels)
    grad_depth = grad_rows.reshape(num_batch, num_rows, num_cols, channels)
    output = (ocean_state.astype(jnp.float32) + mask_float * layer_scale * branch).astype(jnp.bfloat16)
    grad_pad = rim_pad(grad_depth)
    grad_state = (cotangent.astype(jnp.float32) + transposed(grad_pad, dw_kernel, num_rows, num_cols)).astype(jnp.bfloat16)
    factor = 1.0 / jnp.sqrt(jnp.float32(num_batch * num_rows * num_cols))
    grad_kernel = kernel_terms(padded, grad_depth, num_rows, num_cols) * factor
    grad_dw_bias = lax.optimization_barrier(jnp.sum(grad_depth.astype(jnp.float32), axis=(0, 1, 2))) * factor
    grad_w_in, grad_w_out, grad_b_in, grad_b_out, grad_scale, grad_ln_gain, grad_ln_bias = totals
    return (output, grad_state, grad_kernel, grad_dw_bias, grad_ln_gain * factor, grad_ln_bias * factor, grad_w_in * factor, grad_b_in * factor, grad_w_out * factor, grad_b_out * factor, grad_scale * factor)
```

```python
import functools
import jax
import jax.numpy as jnp
from jax import lax
from jax.experimental import pallas as pl
from jax.experimental.pallas import tpu as pltpu
from jax.sharding import PartitionSpec as P

MESH = pl.DeviceIdType.MESH


def phases_of(num_lon, num_lat):
    phases = []
    for axis, size in (("lon", num_lon), ("lat", num_lat)):
        stride = 1
        while stride < size:
            rest = size // stride
            if axis == "lon" and stride == 1 and rest % 2 == 0:
                count = 2
            elif rest % 4 == 0:
                count = 4
            elif rest % 2 == 0:
                count = 2
            else:
                count = rest
            phases.append((axis, stride, count))
            stride *= count
    return phases


def plan(rows, tile, phases):
    steps = []
    for axis, stride, count in phases:
        scatter = rows % (count * tile) == 0
        steps.append((axis, stride, count, scatter, rows))
        if scatter:
            rows //= count
    return steps, rows


def position(axis, stride, count):
    index = lax.axis_index(axis)
    return index, lax.rem(lax.div(index, stride), count)


def partner(axis, stride, count, k):
    index, digit = position(axis, stride, count)
    other = lax.rem(digit + k, count)
    return {axis: index + (other - digit) * stride}, other


class Reducer:
    def __init__(self, tile, steps, mine, whole, landing, send_sem, recv_sem, back_send, back_recv):
        self.tile, self.steps = tile, steps
        self.mine, self.whole, self.landing = mine, whole, landing
        self.send_sem, self.recv_sem = send_sem, recv_sem
        self.back_send, self.back_recv = back_send, back_recv
        self.offsets = [0]
        for axis, stride, count, scatter, rows in steps:
            digit = position(axis, stride, count)[1]
            step = digit * (rows // count) if scatter else 0
            self.offsets.append(self.offsets[-1] + step)

    def span(self, start, rows):
        return pl.ds(pl.multiple_of(start, self.tile), rows)

    def scatter_copies(self, number):
        axis, stride, count, scatter, rows = self.steps[number]
        copies = []
        part = rows // count if scatter else rows
        for k in range(1, count):
            device, other = partner(axis, stride, count, k)
            start = self.offsets[number] + (other * part if scatter else 0)
            copies.append(
                pltpu.make_async_remote_copy(
                    src_ref=self.mine.at[self.span(start, part)],
                    dst_ref=self.landing[number].at[k],
                    send_sem=self.send_sem.at[number, k],
                    recv_sem=self.recv_sem.at[number, k],
                    device_id=device,
                    device_id_type=MESH,
                )
            )
        return copies

    def scatter_start(self, number):
        for copy in self.scatter_copies(number):
            copy.start()

    def scatter_finish(self, number, last):
        axis, stride, count, scatter, rows = self.steps[number]
        digit = position(axis, stride, count)[1]
        for copy in self.scatter_copies(number):
            copy.wait()
        part = rows // count if scatter else rows
        here = self.span(self.offsets[number + 1], part)
        land = self.landing[number]
        if scatter:
            total = self.mine[here].astype(jnp.float32)
            for k in range(1, count):
                total = total + land[k].astype(jnp.float32)
        else:
            land[0] = self.mine[here]
            total = land[digit].astype(jnp.float32)
            for j in range(1, count):
                total = total + land[lax.rem(digit - j + count, count)].astype(jnp.float32)
        target = self.whole if last else self.mine
        target[here] = total.astype(target.dtype)

    def gather_copies(self, number):
        axis, stride, count, scatter, rows = self.steps[number]
        part = rows // count
        here = self.span(self.offsets[number + 1], part)
        copies = []
        for k in range(1, count):
            device, other = partner(axis, stride, count, k)
            copies.append(
                pltpu.make_async_remote_copy(
                    src_ref=self.whole.at[here],
                    dst_ref=self.whole.at[here],
                    send_sem=self.back_send.at[number, k],
                    recv_sem=self.back_recv.at[number, k],
                    device_id=device,
                    device_id_type=MESH,
                )
            )
        return copies

    def gather_start(self, number):
        if self.steps[number][3]:
            for copy in self.gather_copies(number):
                copy.start()

    def gather_finish(self, number):
        if self.steps[number][3]:
            for copy in self.gather_copies(number):
                copy.wait()


def greet(phases):
    barrier = pltpu.get_barrier_semaphore()
    total = 0
    for axis, stride, count in phases:
        for k in range(1, count):
            device, _ = partner(axis, stride, count, k)
            pl.semaphore_signal(barrier, inc=1, device_id=device, device_id_type=MESH)
            total += 1
    pl.semaphore_wait(barrier, total)


def sum_kernel(phases, steps, small_steps, wide_ref, tall_ref, small_ref, wide_out, tall_out, small_out, *scratch):
    num = len(phases)
    mine, whole, small_whole = scratch[:3]
    landing = scratch[3 : 3 + num]
    small_landing = scratch[3 + num : 3 + 2 * num]
    sems = scratch[3 + 2 * num :]
    channels = tall_ref.shape[1]
    depth = wide_ref.shape[0]
    tall = tall_ref.shape[0]
    blocks = wide_ref.shape[1] // channels
    greet(phases)
    mine[0:tall] = tall_ref[...]
    for b in range(blocks):
        mine[tall + b * depth : tall + (b + 1) * depth] = wide_ref[:, b * channels : (b + 1) * channels]
    big = Reducer(16, steps, mine, whole, landing, *sems[:4])
    small = Reducer(8, small_steps, small_ref, small_whole, small_landing, *sems[4:])
    for number in range(num):
        big.scatter_start(number)
        small.scatter_start(number)
        small.scatter_finish(number, number == num - 1)
        big.scatter_finish(number, number == num - 1)
    for number in reversed(range(num)):
        big.gather_start(number)
        small.gather_start(number)
        small.gather_finish(number)
        big.gather_finish(number)
    small_out[...] = small_whole[...]
    tall_out[...] = whole[0:tall]
    for b in range(blocks):
        wide_out[:, b * channels : (b + 1) * channels] = whole[tall + b * depth : tall + (b + 1) * depth]


def summed_over_devices(wide, tall, small):
    phases = phases_of(lax.axis_size("lon"), lax.axis_size("lat"))
    num = len(phases)
    channels = tall.shape[1]
    rows = tall.shape[0] + wide.shape[1] // channels * wide.shape[0]
    steps, _ = plan(rows, 16, phases)
    small_steps, _ = plan(small.shape[0], 8, phases)

    def landings(which, dtype):
        return [
            pltpu.VMEM((count, r // count if scatter else r, channels), dtype)
            for axis, stride, count, scatter, r in which
        ]

    vmem = pl.BlockSpec(memory_space=pltpu.VMEM)

    def body(wide_ref, tall_ref, small_ref, wide_out, tall_out, small_out, small_mine, *scratch):
        small_mine[...] = small_ref[...]
        sum_kernel(phases, steps, small_steps, wide_ref, tall_ref, small_mine, wide_out, tall_out, small_out, *scratch)

    return pl.pallas_call(
        body,
        out_shape=(
            jax.ShapeDtypeStruct(wide.shape, jnp.bfloat16),
            jax.ShapeDtypeStruct(tall.shape, jnp.bfloat16),
            jax.ShapeDtypeStruct(small.shape, jnp.float32),
        ),
        in_specs=[vmem] * 3,
        out_specs=(vmem,) * 3,
        scratch_shapes=[
            pltpu.VMEM(small.shape, jnp.float32),
            pltpu.VMEM((rows, channels), jnp.bfloat16),
            pltpu.VMEM((rows, channels), jnp.bfloat16),
            pltpu.VMEM(small.shape, jnp.float32),
            *landings(steps, jnp.bfloat16),
            *landings(small_steps, jnp.float32),
            *[pltpu.SemaphoreType.DMA((num, 4))] * 8,
        ],
        compiler_params=pltpu.CompilerParams(
            collective_id=0, has_side_effects=True, vmem_limit_bytes=40 * 1024 * 1024
        ),
    )(wide, tall, small)


def extended(array, sides, width, wrap):
    for axis, dim in sides:
        size, length = (lax.axis_size(axis), array.shape[dim])
        up = [(i, (i + 1) % size) for i in range(size if wrap else size - 1)]
        down = [(j, i) for i, j in up]
        last = lax.slice_in_dim(array, length - width, length, axis=dim)
        leading = lax.slice_in_dim(array, 0, width, axis=dim)
        before = lax.ppermute(last, axis, up)
        after = lax.ppermute(leading, axis, down)
        array = jnp.concatenate([before, array, after], axis=dim)
    return array


def depthwise(padded, kernel, num_rows, num_cols):
    summed = jnp.zeros((padded.shape[0], num_rows, num_cols, padded.shape[3]), jnp.float32)
    for row_off in range(7):
        for col_off in range(7):
            summed = (
                summed
                + padded[:, row_off : row_off + num_rows, col_off : col_off + num_cols, :].astype(
                    jnp.float32
                )
                * kernel[row_off, col_off]
            )
    return summed


def transposed(padded, kernel, num_rows, num_cols):
    summed = jnp.zeros((padded.shape[0], num_rows, num_cols, padded.shape[3]), jnp.float32)
    for row_off in range(7):
        for col_off in range(7):
            summed = (
                summed
                + padded[
                    :, 6 - row_off : 6 - row_off + num_rows, 6 - col_off : 6 - col_off + num_cols, :
                ].astype(jnp.float32)
                * kernel[row_off, col_off]
            )
    return summed


def kernel_terms(padded, grad_depth, num_rows, num_cols):
    grad_float = grad_depth.astype(jnp.float32)
    rows_out = []
    for row_off in range(7):
        cols_out = []
        for col_off in range(7):
            window = padded[
                :, row_off : row_off + num_rows, col_off : col_off + num_cols, :
            ].astype(jnp.float32)
            cols_out.append(jnp.sum(window * grad_float, axis=(0, 1, 2)))
        rows_out.append(jnp.stack(cols_out))
    return jnp.stack(rows_out)


def forward_tokens(depth_out, ln_gain, ln_bias, w_in, b_in, w_out, b_out):
    center = depth_out - jnp.mean(depth_out, axis=-1, keepdims=True)
    inv_std = lax.rsqrt(jnp.mean(center * center, axis=-1, keepdims=True) + 1e-06)
    norm_hat = center * inv_std
    normed = (norm_hat * ln_gain + ln_bias).astype(jnp.bfloat16)
    pre_act = jnp.dot(normed, w_in, preferred_element_type=jnp.float32) + b_in
    activated = jax.nn.gelu(pre_act, approximate=True).astype(jnp.bfloat16)
    branch = jnp.dot(activated, w_out, preferred_element_type=jnp.float32) + b_out
    return (norm_hat, inv_std, normed, pre_act, activated, branch)


def backward_tokens(masked, norm_hat, inv_std, pre_act, ln_gain, w_in, w_out, layer_scale):
    grad_branch = (masked * layer_scale).astype(jnp.bfloat16)
    grad_act = lax.dot_general(
        grad_branch, w_out, (((1,), (1,)), ((), ())), preferred_element_type=jnp.float32
    )
    unused, pull_back = jax.vjp(lambda v: jax.nn.gelu(v, approximate=True), pre_act)
    grad_pre = pull_back(grad_act)[0].astype(jnp.bfloat16)
    grad_norm = lax.dot_general(
        grad_pre, w_in, (((1,), (1,)), ((), ())), preferred_element_type=jnp.float32
    )
    scaled = grad_norm * ln_gain
    grad_depth = (
        inv_std
        * (
            scaled
            - jnp.mean(scaled, axis=-1, keepdims=True)
            - norm_hat * jnp.mean(scaled * norm_hat, axis=-1, keepdims=True)
        )
    ).astype(jnp.bfloat16)
    return (grad_branch, grad_pre, grad_norm, grad_depth)


def weight_terms(masked, branch, grad_branch, activated, normed, grad_pre, grad_norm, norm_hat):
    dims = (((0,), (0,)), ((), ()))
    grad_w_in = lax.dot_general(normed, grad_pre, dims, preferred_element_type=jnp.float32)
    grad_w_out = lax.dot_general(activated, grad_branch, dims, preferred_element_type=jnp.float32)
    return (
        grad_w_in,
        grad_w_out,
        jnp.sum(grad_pre.astype(jnp.float32), axis=0),
        jnp.sum(grad_branch.astype(jnp.float32), axis=0),
        jnp.sum(masked * branch, axis=0),
        jnp.sum(grad_norm * norm_hat, axis=0),
        jnp.sum(grad_norm, axis=0),
    )


def local(
    ocean_state,
    land_sea,
    cotangent,
    dw_kernel,
    dw_bias,
    ln_gain,
    ln_bias,
    w_in,
    b_in,
    w_out,
    b_out,
    layer_scale,
):
    num_batch, num_rows, num_cols, channels = ocean_state.shape
    mask_float = land_sea.astype(jnp.float32)[..., None]
    lon_ext = extended(ocean_state, (("lon", 2),), 3, True)
    padded = extended(lon_ext, (("lat", 1),), 3, False)
    depth_out = depthwise(padded, dw_kernel, num_rows, num_cols) + dw_bias
    masked = (mask_float * cotangent.astype(jnp.float32)).reshape(-1, channels)
    norm_hat, inv_std, normed, pre_act, activated, branch = forward_tokens(
        depth_out.reshape(-1, channels), ln_gain, ln_bias, w_in, b_in, w_out, b_out
    )
    grad_branch, grad_pre, grad_norm, grad_flat = backward_tokens(
        masked, norm_hat, inv_std, pre_act, ln_gain, w_in, w_out, layer_scale
    )
    grad_terms = weight_terms(
        masked, branch, grad_branch, activated, normed, grad_pre, grad_norm, norm_hat
    )
    grad_depth = grad_flat.reshape(num_batch, num_rows, num_cols, channels)
    grad_ext = extended(grad_depth, (("lon", 2),), 3, True)
    grad_pad = extended(grad_ext, (("lat", 1),), 3, False)
    branch_own = branch.reshape(num_batch, num_rows, num_cols, channels)
    output = (ocean_state.astype(jnp.float32) + mask_float * layer_scale * branch_own).astype(
        jnp.bfloat16
    )
    grad_state = (
        cotangent.astype(jnp.float32) + transposed(grad_pad, dw_kernel, num_rows, num_cols)
    ).astype(jnp.bfloat16)
    kernel_part = kernel_terms(padded, grad_depth, num_rows, num_cols)
    bias_part = jnp.sum(grad_depth.astype(jnp.float32), axis=(0, 1, 2))
    grad_w_in, grad_w_out, grad_b_in, grad_b_out, grad_scale, grad_ln_gain, grad_ln_bias = (
        grad_terms
    )
    rows = [
        kernel_part.reshape(-1, channels),
        bias_part[None],
        grad_ln_gain[None],
        grad_ln_bias[None],
        grad_b_out[None],
        grad_scale[None],
        grad_b_in.reshape(-1, channels),
    ]
    used = sum(r.shape[0] for r in rows)
    small = jnp.concatenate(rows + [jnp.zeros((-used % 64, channels), jnp.float32)])
    grad_w_in, grad_w_out, small = summed_over_devices(
        grad_w_in.astype(jnp.bfloat16), grad_w_out.astype(jnp.bfloat16), small
    )
    grad_w_in, grad_w_out = (grad_w_in.astype(jnp.float32), grad_w_out.astype(jnp.float32))
    all_cells = num_batch * num_rows * num_cols * lax.axis_size("lon") * lax.axis_size("lat")
    factor = 1.0 / jnp.sqrt(jnp.float32(all_cells))
    small = small * factor
    return (
        output,
        grad_state,
        small[:49].reshape(7, 7, channels),
        small[49],
        small[50],
        small[51],
        grad_w_in * factor,
        small[54 : 54 + b_in.shape[0] // channels].reshape(-1),
        grad_w_out * factor,
        small[52],
        small[53],
    )


def solution(mesh):
    in_specs = (
        P(None, "lat", "lon", None),
        P(None, "lat", "lon"),
        P(None, "lat", "lon", None),
        P(),
        P(),
        P(),
        P(),
        P(),
        P(),
        P(),
        P(),
        P(),
    )
    out_specs = (
        P(None, "lat", "lon", None),
        P(None, "lat", "lon", None),
        P(),
        P(),
        P(),
        P(),
        P(),
        P(),
        P(),
        P(),
        P(),
    )
    return jax.shard_map(local, mesh=mesh, in_specs=in_specs, out_specs=out_specs, check_vma=False)
```

```python
import functools
import jax
import jax.numpy as jnp
from jax import lax
from jax.experimental import pallas as pl
from jax.experimental.pallas import tpu as pltpu
from jax.sharding import PartitionSpec as P

MESH = pl.DeviceIdType.MESH


def phases_of(num_lon, num_lat):
    phases = []
    for axis, size in (("lon", num_lon), ("lat", num_lat)):
        stride = 1
        while stride < size:
            rest = size // stride
            if axis == "lon" and stride == 1 and rest % 2 == 0:
                count = 2
            elif rest % 4 == 0:
                count = 4
            elif rest % 2 == 0:
                count = 2
            else:
                count = rest
            phases.append((axis, stride, count))
            stride *= count
    return phases


def plan(rows, tile, phases):
    steps = []
    for axis, stride, count in phases:
        scatter = rows % (count * tile) == 0
        steps.append((axis, stride, count, scatter, rows))
        if scatter:
            rows //= count
    return steps, rows


def position(axis, stride, count):
    index = lax.axis_index(axis)
    return index, lax.rem(lax.div(index, stride), count)


def partner(axis, stride, count, k):
    index, digit = position(axis, stride, count)
    other = lax.rem(digit + k, count)
    return {axis: index + (other - digit) * stride}, other


class Reducer:
    def __init__(self, tile, steps, mine, whole, landing, send_sem, recv_sem, back_send, back_recv):
        self.tile, self.steps = tile, steps
        self.mine, self.whole, self.landing = mine, whole, landing
        self.send_sem, self.recv_sem = send_sem, recv_sem
        self.back_send, self.back_recv = back_send, back_recv
        self.offsets = [0]
        for axis, stride, count, scatter, rows in steps:
            digit = position(axis, stride, count)[1]
            step = digit * (rows // count) if scatter else 0
            self.offsets.append(self.offsets[-1] + step)

    def span(self, start, rows):
        return pl.ds(pl.multiple_of(start, self.tile), rows)

    def scatter_copies(self, number):
        axis, stride, count, scatter, rows = self.steps[number]
        copies = []
        part = rows // count if scatter else rows
        for k in range(1, count):
            device, other = partner(axis, stride, count, k)
            start = self.offsets[number] + (other * part if scatter else 0)
            copies.append(
                pltpu.make_async_remote_copy(
                    src_ref=self.mine.at[self.span(start, part)],
                    dst_ref=self.landing[number].at[k],
                    send_sem=self.send_sem.at[number, k],
                    recv_sem=self.recv_sem.at[number, k],
                    device_id=device,
                    device_id_type=MESH,
                )
            )
        return copies

    def scatter_start(self, number):
        for copy in self.scatter_copies(number):
            copy.start()

    def scatter_finish(self, number, last):
        axis, stride, count, scatter, rows = self.steps[number]
        digit = position(axis, stride, count)[1]
        for copy in self.scatter_copies(number):
            copy.wait()
        part = rows // count if scatter else rows
        here = self.span(self.offsets[number + 1], part)
        land = self.landing[number]
        if scatter:
            total = self.mine[here].astype(jnp.float32)
            for k in range(1, count):
                total = total + land[k].astype(jnp.float32)
        else:
            land[0] = self.mine[here]
            total = land[digit].astype(jnp.float32)
            for j in range(1, count):
                total = total + land[lax.rem(digit - j + count, count)].astype(jnp.float32)
        target = self.whole if last else self.mine
        target[here] = total.astype(target.dtype)

    def gather_copies(self, number):
        axis, stride, count, scatter, rows = self.steps[number]
        part = rows // count
        here = self.span(self.offsets[number + 1], part)
        copies = []
        for k in range(1, count):
            device, other = partner(axis, stride, count, k)
            copies.append(
                pltpu.make_async_remote_copy(
                    src_ref=self.whole.at[here],
                    dst_ref=self.whole.at[here],
                    send_sem=self.back_send.at[number, k],
                    recv_sem=self.back_recv.at[number, k],
                    device_id=device,
                    device_id_type=MESH,
                )
            )
        return copies

    def gather_start(self, number):
        if self.steps[number][3]:
            for copy in self.gather_copies(number):
                copy.start()

    def gather_finish(self, number):
        if self.steps[number][3]:
            for copy in self.gather_copies(number):
                copy.wait()


def greet(phases):
    barrier = pltpu.get_barrier_semaphore()
    total = 0
    for axis, stride, count in phases:
        for k in range(1, count):
            device, _ = partner(axis, stride, count, k)
            pl.semaphore_signal(barrier, inc=1, device_id=device, device_id_type=MESH)
            total += 1
    return total


SIDES = [(dy, dx) for dy in (-1, 0, 1) for dx in (-1, 0, 1) if (dy, dx) != (0, 0)]
EDGE = 16


def on_grid(dy):
    there = lax.axis_index("lat") + dy
    return (there >= 0) & (there < lax.axis_size("lat"))


def neighbour(dy, dx):
    num_lon = lax.axis_size("lon")
    return {
        "lat": lax.axis_index("lat") + dy,
        "lon": lax.rem(lax.axis_index("lon") + dx + num_lon, num_lon),
    }


def greet_neighbours(others):
    barrier = pltpu.get_barrier_semaphore()
    for dy in (-1, 0, 1):

        @pl.when(on_grid(dy))
        def _():
            sides = [s for s in SIDES if s[0] == dy]
            for side in sides:
                pl.semaphore_signal(
                    barrier, inc=1, device_id=neighbour(*side), device_id_type=MESH
                )

    lat, num_lat = lax.axis_index("lat"), lax.axis_size("lat")
    around = jnp.minimum(lat, 1) + jnp.minimum(num_lat - 1 - lat, 1)
    pl.semaphore_wait(barrier, others + 2 + 3 * around)


class Halo:
    def __init__(self, block, lands, send_sem, recv_sem):
        self.block, self.lands = block, dict(zip(SIDES, lands))
        self.send_sem, self.recv_sem = send_sem, recv_sem

    def copy(self, side):
        dy, dx = side
        rows, cols, _ = self.block.shape
        row = {1: pl.ds(rows - 3, 3), 0: pl.ds(0, rows), -1: pl.ds(0, 3)}[dy]
        col = {1: pl.ds(cols - EDGE, EDGE), 0: pl.ds(0, cols), -1: pl.ds(0, EDGE)}[dx]
        number = SIDES.index(side)
        return pltpu.make_async_remote_copy(
            src_ref=self.block.at[row, col],
            dst_ref=self.lands[side],
            send_sem=self.send_sem.at[number],
            recv_sem=self.recv_sem.at[number],
            device_id=neighbour(dy, dx),
            device_id_type=MESH,
        )

    def each(self, sign, act):
        for dy in (-1, 0, 1):

            @pl.when(on_grid(sign * dy))
            def _():
                for side in SIDES:
                    if side[0] == dy:
                        act(self.copy(side))

    def start(self):
        self.each(1, lambda copy: copy.start())

    def finish(self, pad):
        self.each(-1, lambda copy: copy.wait_recv())
        self.each(1, lambda copy: copy.wait_send())
        rows, cols, channels = self.block.shape
        for dy, first, count in ((1, 0, 3), (0, 3, rows), (-1, rows + 3, 3)):

            @pl.when(on_grid(-dy))
            def _():
                middle = self.block if dy == 0 else self.lands[dy, 0]
                here = pl.ds(first, count)
                pad[here, 8 : 8 + cols] = middle[...].astype(jnp.float32)
                left = self.lands[dy, 1][...].astype(jnp.float32)
                right = self.lands[dy, -1][...].astype(jnp.float32)
                pad[here, 0:8] = left[:, EDGE - 8 :]
                pad[here, 8 + cols : 16 + cols] = right[:, :8]

            if dy != 0:

                @pl.when(jnp.logical_not(on_grid(-dy)))
                def _():
                    pad[pl.ds(first, count)] = jnp.zeros((count, cols + 16, channels), jnp.float32)


def halo_scratch(rows, cols, channels):
    lands = [
        pltpu.VMEM((3 if dy else rows, EDGE if dx else cols, channels), jnp.bfloat16)
        for dy, dx in SIDES
    ]
    return lands + [pltpu.SemaphoreType.DMA((8,))] * 2


def convolve(pad, taps, begin, first, last, flip, store):
    cols, channels = pad.shape[1] - 16, pad.shape[2]

    def row_step(p, carry):
        for h in range(channels // 128):
            lanes = slice(h * 128, (h + 1) * 128)
            total = begin(p, lanes)
            for i in range(7):
                for j in range(7):
                    t = i * 7 + j
                    t = 48 - t if flip else t
                    total = total + pad[p + i, 5 + j : 5 + j + cols, lanes] * taps[t : t + 1, lanes]
            store(p, lanes, total)
        return carry

    lax.fori_loop(first, last, row_step, 0)


def correlate(pad, grad, out):
    rows, cols, channels = grad.shape
    for h in range(channels // 128):
        lanes = slice(h * 128, (h + 1) * 128)
        for j in range(7):

            def row_step(p, sums):
                own = grad[p, :, lanes].astype(jnp.float32)
                new = []
                for i in range(7):
                    term = pad[p + i, 5 + j : 5 + j + cols, lanes] * own
                    new.append(sums[i] + jnp.sum(term.reshape(cols // 8, 8, 128), axis=0))
                return tuple(new)

            sums = lax.fori_loop(
                0, rows, row_step, tuple(jnp.zeros((8, 128), jnp.float32) for _ in range(7))
            )
            for i in range(7):
                out[i * 7 + j : i * 7 + j + 1, lanes] = jnp.sum(sums[i], axis=0, keepdims=True)


def depth_kernel(state, taps, bias, depth_out, pad, *scratch):
    halo = Halo(state, scratch[:8], *scratch[8:])
    greet_neighbours(0)
    halo.start()
    halo.finish(pad)
    cols = state.shape[1]

    def begin(p, lanes):
        return jnp.broadcast_to(bias[:, lanes], (cols, 128))

    def store(p, lanes, total):
        depth_out[p, :, lanes] = total

    convolve(pad, taps, begin, 0, state.shape[0], False, store)


def depth_of(state, taps, bias):
    rows, cols, channels = state.shape
    vmem = pl.BlockSpec(memory_space=pltpu.VMEM)
    return pl.pallas_call(
        depth_kernel,
        out_shape=(
            jax.ShapeDtypeStruct(state.shape, jnp.float32),
            jax.ShapeDtypeStruct((rows + 6, cols + 16, channels), jnp.float32),
        ),
        in_specs=[vmem] * 3,
        out_specs=(vmem,) * 2,
        scratch_shapes=halo_scratch(rows, cols, channels),
        compiler_params=pltpu.CompilerParams(
            collective_id=1, has_side_effects=True, vmem_limit_bytes=40 * 1024 * 1024
        ),
    )(state, taps, bias[None])


def final_kernel(phases, steps, small_steps, wide_ref, tall_ref, other_ref, grad_ref, pad_ref, cot_ref,
                 taps_ref, wide_out, tall_out, small_out, state_out, *scratch):
    num = len(phases)
    small_mine, mine, whole, small_whole, grad_pad = scratch[:5]
    scratch = scratch[5:]
    halo = Halo(grad_ref, scratch[:8], *scratch[8:10])
    landing = scratch[10 : 10 + num]
    small_landing = scratch[10 + num : 10 + 2 * num]
    sems = scratch[10 + 2 * num :]
    channels = tall_ref.shape[1]
    depth = wide_ref.shape[0]
    tall = tall_ref.shape[0]
    blocks = wide_ref.shape[1] // channels
    rows = grad_ref.shape[0]
    greet_neighbours(greet(phases))
    halo.start()
    mine[0:tall] = tall_ref[...]
    for b in range(blocks):
        mine[tall + b * depth : tall + (b + 1) * depth] = wide_ref[:, b * channels : (b + 1) * channels]
    big = Reducer(16, steps, mine, whole, landing, *sems[:4])
    small = Reducer(8, small_steps, small_mine, small_whole, small_landing, *sems[4:])

    def small_terms():
        used = 49 + other_ref.shape[0]
        small_mine[49:used] = other_ref[...]
        if used < small_mine.shape[0]:
            small_mine[used:] = jnp.zeros((small_mine.shape[0] - used, channels), jnp.float32)
        correlate(pad_ref, grad_ref, small_mine)

    def begin(p, lanes):
        return cot_ref[p, :, lanes].astype(jnp.float32)

    def store(p, lanes, total):
        state_out[p, :, lanes] = total.astype(jnp.bfloat16)

    def near_rows():
        halo.finish(grad_pad)
        convolve(grad_pad, taps_ref, begin, 0, rows // 2, True, store)

    def far_rows():
        convolve(grad_pad, taps_ref, begin, rows // 2, rows, True, store)

    def chain(reducer):
        moves = []
        for n in range(num):
            moves.append(
                (
                    functools.partial(reducer.scatter_start, n),
                    functools.partial(reducer.scatter_finish, n, n == num - 1),
                )
            )
        for n in reversed(range(num)):
            if reducer.steps[n][3]:
                moves.append(
                    (
                        functools.partial(reducer.gather_start, n),
                        functools.partial(reducer.gather_finish, n),
                    )
                )
        return moves

    lag = 2
    big_moves, small_moves = chain(big), chain(small)
    beside = {1: small_terms, 2: near_rows, 3: far_rows}
    for t in range(max(len(big_moves), len(small_moves) + lag)):
        moves = []
        if 0 <= t - lag < len(small_moves):
            moves.append(small_moves[t - lag])
        if t < len(big_moves):
            moves.append(big_moves[t])
        for start, _ in reversed(moves):
            start()
        if t in beside:
            beside[t]()
        for _, finish in moves:
            finish()
    small_out[...] = small_whole[...]
    tall_out[...] = whole[0:tall]
    for b in range(blocks):
        wide_out[:, b * channels : (b + 1) * channels] = whole[tall + b * depth : tall + (b + 1) * depth]


def final_of(wide, tall, other, grad, pad, cot, taps):
    phases = phases_of(lax.axis_size("lon"), lax.axis_size("lat"))
    num = len(phases)
    channels = tall.shape[1]
    rows = tall.shape[0] + wide.shape[1] // channels * wide.shape[0]
    small_rows = -(-(49 + other.shape[0]) // 64) * 64
    steps, _ = plan(rows, 16, phases)
    small_steps, _ = plan(small_rows, 8, phases)

    def landings(which, dtype):
        return [
            pltpu.VMEM((count, r // count if scatter else r, channels), dtype)
            for axis, stride, count, scatter, r in which
        ]

    vmem = pl.BlockSpec(memory_space=pltpu.VMEM)
    small = (small_rows, channels)
    return pl.pallas_call(
        functools.partial(final_kernel, phases, steps, small_steps),
        out_shape=(
            jax.ShapeDtypeStruct(wide.shape, jnp.bfloat16),
            jax.ShapeDtypeStruct(tall.shape, jnp.bfloat16),
            jax.ShapeDtypeStruct(small, jnp.float32),
            jax.ShapeDtypeStruct(grad.shape, jnp.bfloat16),
        ),
        in_specs=[vmem] * 7,
        out_specs=(vmem,) * 4,
        scratch_shapes=[
            pltpu.VMEM(small, jnp.float32),
            pltpu.VMEM((rows, channels), jnp.bfloat16),
            pltpu.VMEM((rows, channels), jnp.bfloat16),
            pltpu.VMEM(small, jnp.float32),
            pltpu.VMEM(pad.shape, jnp.float32),
            *halo_scratch(*grad.shape),
            *landings(steps, jnp.bfloat16),
            *landings(small_steps, jnp.float32),
            *[pltpu.SemaphoreType.DMA((num, 4))] * 8,
        ],
        compiler_params=pltpu.CompilerParams(
            collective_id=0, has_side_effects=True, vmem_limit_bytes=40 * 1024 * 1024
        ),
    )(wide, tall, other, grad, pad, cot, taps)


def forward_tokens(depth_out, ln_gain, ln_bias, w_in, b_in, w_out, b_out):
    center = depth_out - jnp.mean(depth_out, axis=-1, keepdims=True)
    inv_std = lax.rsqrt(jnp.mean(center * center, axis=-1, keepdims=True) + 1e-06)
    norm_hat = center * inv_std
    normed = (norm_hat * ln_gain + ln_bias).astype(jnp.bfloat16)
    pre_act = jnp.dot(normed, w_in, preferred_element_type=jnp.float32) + b_in
    activated = jax.nn.gelu(pre_act, approximate=True).astype(jnp.bfloat16)
    branch = jnp.dot(activated, w_out, preferred_element_type=jnp.float32) + b_out
    return (norm_hat, inv_std, normed, pre_act, activated, branch)


def backward_tokens(masked, norm_hat, inv_std, pre_act, ln_gain, w_in, w_out, layer_scale):
    grad_branch = (masked * layer_scale).astype(jnp.bfloat16)
    grad_act = lax.dot_general(
        grad_branch, w_out, (((1,), (1,)), ((), ())), preferred_element_type=jnp.float32
    )
    unused, pull_back = jax.vjp(lambda v: jax.nn.gelu(v, approximate=True), pre_act)
    grad_pre = pull_back(grad_act)[0].astype(jnp.bfloat16)
    grad_norm = lax.dot_general(
        grad_pre, w_in, (((1,), (1,)), ((), ())), preferred_element_type=jnp.float32
    )
    scaled = grad_norm * ln_gain
    grad_depth = (
        inv_std
        * (
            scaled
            - jnp.mean(scaled, axis=-1, keepdims=True)
            - norm_hat * jnp.mean(scaled * norm_hat, axis=-1, keepdims=True)
        )
    ).astype(jnp.bfloat16)
    return (grad_branch, grad_pre, grad_norm, grad_depth)


def weight_terms(masked, branch, grad_branch, activated, normed, grad_pre, grad_norm, norm_hat):
    dims = (((0,), (0,)), ((), ()))
    grad_w_in = lax.dot_general(normed, grad_pre, dims, preferred_element_type=jnp.float32)
    grad_w_out = lax.dot_general(activated, grad_branch, dims, preferred_element_type=jnp.float32)
    return (
        grad_w_in,
        grad_w_out,
        jnp.sum(grad_pre.astype(jnp.float32), axis=0),
        jnp.sum(grad_branch.astype(jnp.float32), axis=0),
        jnp.sum(masked * branch, axis=0),
        jnp.sum(grad_norm * norm_hat, axis=0),
        jnp.sum(grad_norm, axis=0),
    )


def local(
    ocean_state,
    land_sea,
    cotangent,
    dw_kernel,
    dw_bias,
    ln_gain,
    ln_bias,
    w_in,
    b_in,
    w_out,
    b_out,
    layer_scale,
):
    num_batch, num_rows, num_cols, channels = ocean_state.shape
    mask_float = land_sea.astype(jnp.float32)[..., None]
    taps = dw_kernel.reshape(-1, channels)
    depth_out, padded = depth_of(ocean_state[0], taps, dw_bias)
    masked = (mask_float * cotangent.astype(jnp.float32)).reshape(-1, channels)
    norm_hat, inv_std, normed, pre_act, activated, branch = forward_tokens(
        depth_out.reshape(-1, channels), ln_gain, ln_bias, w_in, b_in, w_out, b_out
    )
    grad_branch, grad_pre, grad_norm, grad_flat = backward_tokens(
        masked, norm_hat, inv_std, pre_act, ln_gain, w_in, w_out, layer_scale
    )
    grad_terms = weight_terms(
        masked, branch, grad_branch, activated, normed, grad_pre, grad_norm, norm_hat
    )
    grad_depth = grad_flat.reshape(num_batch, num_rows, num_cols, channels)
    branch_own = branch.reshape(num_batch, num_rows, num_cols, channels)
    output = (ocean_state.astype(jnp.float32) + mask_float * layer_scale * branch_own).astype(
        jnp.bfloat16
    )
    bias_part = jnp.sum(grad_depth.astype(jnp.float32), axis=(0, 1, 2))
    grad_w_in, grad_w_out, grad_b_in, grad_b_out, grad_scale, grad_ln_gain, grad_ln_bias = (
        grad_terms
    )
    rows = [
        bias_part[None],
        grad_ln_gain[None],
        grad_ln_bias[None],
        grad_b_out[None],
        grad_scale[None],
        grad_b_in.reshape(-1, channels),
    ]
    grad_w_in, grad_w_out, small, grad_state = final_of(
        grad_w_in.astype(jnp.bfloat16),
        grad_w_out.astype(jnp.bfloat16),
        jnp.concatenate(rows),
        grad_depth[0],
        padded,
        cotangent[0],
        taps,
    )
    grad_state = grad_state[None]
    grad_w_in, grad_w_out = (grad_w_in.astype(jnp.float32), grad_w_out.astype(jnp.float32))
    all_cells = num_batch * num_rows * num_cols * lax.axis_size("lon") * lax.axis_size("lat")
    factor = 1.0 / jnp.sqrt(jnp.float32(all_cells))
    small = small * factor
    return (
        output,
        grad_state,
        small[:49].reshape(7, 7, channels),
        small[49],
        small[50],
        small[51],
        grad_w_in * factor,
        small[54 : 54 + b_in.shape[0] // channels].reshape(-1),
        grad_w_out * factor,
        small[52],
        small[53],
    )


def solution(mesh):
    in_specs = (
        P(None, "lat", "lon", None),
        P(None, "lat", "lon"),
        P(None, "lat", "lon", None),
        P(),
        P(),
        P(),
        P(),
        P(),
        P(),
        P(),
        P(),
        P(),
    )
    out_specs = (
        P(None, "lat", "lon", None),
        P(None, "lat", "lon", None),
        P(),
        P(),
        P(),
        P(),
        P(),
        P(),
        P(),
        P(),
        P(),
    )
    return jax.shard_map(local, mesh=mesh, in_specs=in_specs, out_specs=out_specs, check_vma=False)
```

```python
import functools
import jax
import jax.numpy as jnp
from jax import lax
from jax.experimental import pallas as pl
from jax.experimental.pallas import tpu as pltpu
from jax.sharding import PartitionSpec as P

MESH = pl.DeviceIdType.MESH


def phases_of(num_lon, num_lat):
    phases = []
    for axis, size in (("lon", num_lon), ("lat", num_lat)):
        stride = 1
        while stride < size:
            rest = size // stride
            if axis == "lon" and stride == 1 and rest % 2 == 0:
                count = 2
            elif rest % 4 == 0:
                count = 4
            elif rest % 2 == 0:
                count = 2
            else:
                count = rest
            phases.append((axis, stride, count))
            stride *= count
    return phases


def plan(rows, tile, phases):
    steps = []
    for axis, stride, count in phases:
        scatter = rows % (count * tile) == 0
        steps.append((axis, stride, count, scatter, rows))
        if scatter:
            rows //= count
    return steps, rows


def position(axis, stride, count):
    index = lax.axis_index(axis)
    return index, lax.rem(lax.div(index, stride), count)


def partner(axis, stride, count, k):
    index, digit = position(axis, stride, count)
    other = lax.rem(digit + k, count)
    return {axis: index + (other - digit) * stride}, other


class Reducer:
    def __init__(self, tile, steps, mine, whole, landing, send_sem, recv_sem, back_send, back_recv):
        self.tile, self.steps = tile, steps
        self.mine, self.whole, self.landing = mine, whole, landing
        self.send_sem, self.recv_sem = send_sem, recv_sem
        self.back_send, self.back_recv = back_send, back_recv
        self.offsets = [0]
        for axis, stride, count, scatter, rows in steps:
            digit = position(axis, stride, count)[1]
            step = digit * (rows // count) if scatter else 0
            self.offsets.append(self.offsets[-1] + step)

    def span(self, start, rows):
        return pl.ds(pl.multiple_of(start, self.tile), rows)

    def scatter_copies(self, number):
        axis, stride, count, scatter, rows = self.steps[number]
        copies = []
        part = rows // count if scatter else rows
        for k in range(1, count):
            device, other = partner(axis, stride, count, k)
            start = self.offsets[number] + (other * part if scatter else 0)
            copies.append(
                pltpu.make_async_remote_copy(
                    src_ref=self.mine.at[self.span(start, part)],
                    dst_ref=self.landing[number].at[k],
                    send_sem=self.send_sem.at[number, k],
                    recv_sem=self.recv_sem.at[number, k],
                    device_id=device,
                    device_id_type=MESH,
                )
            )
        return copies

    def scatter_start(self, number):
        for copy in self.scatter_copies(number):
            copy.start()

    def scatter_finish(self, number, last):
        axis, stride, count, scatter, rows = self.steps[number]
        digit = position(axis, stride, count)[1]
        for copy in self.scatter_copies(number):
            copy.wait()
        part = rows // count if scatter else rows
        here = self.span(self.offsets[number + 1], part)
        land = self.landing[number]
        if scatter:
            total = self.mine[here].astype(jnp.float32)
            for k in range(1, count):
                total = total + land[k].astype(jnp.float32)
        else:
            land[0] = self.mine[here]
            total = land[digit].astype(jnp.float32)
            for j in range(1, count):
                total = total + land[lax.rem(digit - j + count, count)].astype(jnp.float32)
        target = self.whole if last else self.mine
        target[here] = total.astype(target.dtype)

    def gather_copies(self, number):
        axis, stride, count, scatter, rows = self.steps[number]
        part = rows // count
        here = self.span(self.offsets[number + 1], part)
        copies = []
        for k in range(1, count):
            device, other = partner(axis, stride, count, k)
            copies.append(
                pltpu.make_async_remote_copy(
                    src_ref=self.whole.at[here],
                    dst_ref=self.whole.at[here],
                    send_sem=self.back_send.at[number, k],
                    recv_sem=self.back_recv.at[number, k],
                    device_id=device,
                    device_id_type=MESH,
                )
            )
        return copies

    def gather_start(self, number):
        if self.steps[number][3]:
            for copy in self.gather_copies(number):
                copy.start()

    def gather_finish(self, number):
        if self.steps[number][3]:
            for copy in self.gather_copies(number):
                copy.wait()


def greet(phases):
    barrier = pltpu.get_barrier_semaphore()
    total = 0
    for axis, stride, count in phases:
        for k in range(1, count):
            device, _ = partner(axis, stride, count, k)
            pl.semaphore_signal(barrier, inc=1, device_id=device, device_id_type=MESH)
            total += 1
    return total


SIDES = [(dy, dx) for dy in (-1, 0, 1) for dx in (-1, 0, 1) if (dy, dx) != (0, 0)]
EDGE = 16


def on_grid(dy):
    there = lax.axis_index("lat") + dy
    return (there >= 0) & (there < lax.axis_size("lat"))


def neighbour(dy, dx):
    num_lon = lax.axis_size("lon")
    return {
        "lat": lax.axis_index("lat") + dy,
        "lon": lax.rem(lax.axis_index("lon") + dx + num_lon, num_lon),
    }


def greet_neighbours(others):
    barrier = pltpu.get_barrier_semaphore()
    for dy in (-1, 0, 1):

        @pl.when(on_grid(dy))
        def _():
            sides = [s for s in SIDES if s[0] == dy]
            for side in sides:
                pl.semaphore_signal(
                    barrier, inc=1, device_id=neighbour(*side), device_id_type=MESH
                )

    lat, num_lat = lax.axis_index("lat"), lax.axis_size("lat")
    around = jnp.minimum(lat, 1) + jnp.minimum(num_lat - 1 - lat, 1)
    pl.semaphore_wait(barrier, others + 2 + 3 * around)


class Halo:
    def __init__(self, block, lands, send_sem, recv_sem):
        self.block, self.lands = block, dict(zip(SIDES, lands))
        self.send_sem, self.recv_sem = send_sem, recv_sem

    def copy(self, side):
        dy, dx = side
        rows, cols, _ = self.block.shape
        row = {1: pl.ds(rows - 3, 3), 0: pl.ds(0, rows), -1: pl.ds(0, 3)}[dy]
        col = {1: pl.ds(cols - EDGE, EDGE), 0: pl.ds(0, cols), -1: pl.ds(0, EDGE)}[dx]
        number = SIDES.index(side)
        return pltpu.make_async_remote_copy(
            src_ref=self.block.at[row, col],
            dst_ref=self.lands[side],
            send_sem=self.send_sem.at[number],
            recv_sem=self.recv_sem.at[number],
            device_id=neighbour(dy, dx),
            device_id_type=MESH,
        )

    def each(self, sign, act):
        for dy in (-1, 0, 1):

            @pl.when(on_grid(sign * dy))
            def _():
                for side in SIDES:
                    if side[0] == dy:
                        act(self.copy(side))

    def start(self):
        self.each(1, lambda copy: copy.start())

    def finish(self, pad):
        self.each(-1, lambda copy: copy.wait_recv())
        self.each(1, lambda copy: copy.wait_send())
        rows, cols, channels = self.block.shape
        for dy, first, count in ((1, 0, 3), (0, 3, rows), (-1, rows + 3, 3)):

            @pl.when(on_grid(-dy))
            def _():
                middle = self.block if dy == 0 else self.lands[dy, 0]
                here = pl.ds(first, count)
                pad[here, 8 : 8 + cols] = middle[...].astype(jnp.float32)
                left = self.lands[dy, 1][...].astype(jnp.float32)
                right = self.lands[dy, -1][...].astype(jnp.float32)
                pad[here, 0:8] = left[:, EDGE - 8 :]
                pad[here, 8 + cols : 16 + cols] = right[:, :8]

            if dy != 0:

                @pl.when(jnp.logical_not(on_grid(-dy)))
                def _():
                    pad[pl.ds(first, count)] = jnp.zeros((count, cols + 16, channels), jnp.float32)


def halo_scratch(rows, cols, channels):
    lands = [
        pltpu.VMEM((3 if dy else rows, EDGE if dx else cols, channels), jnp.bfloat16)
        for dy, dx in SIDES
    ]
    return lands + [pltpu.SemaphoreType.DMA((8,))] * 2


def shift_columns(pad, shifted):
    cols = shifted.shape[2]

    def row_step(r, carry):
        for j in range(7):
            shifted[j, r] = pad[r, 5 + j : 5 + j + cols]
        return carry

    lax.fori_loop(0, pad.shape[0], row_step, 0)


def shifted_scratch(rows, cols, channels):
    return pltpu.VMEM((7, rows + 6, cols, channels), jnp.float32)


def convolve(shifted, taps, begin, first, last, flip, store):
    channels = shifted.shape[3]

    def row_step(p, carry):
        for h in range(channels // 128):
            lanes = slice(h * 128, (h + 1) * 128)
            total = begin(p, lanes)
            for i in range(7):
                for j in range(7):
                    t = i * 7 + j
                    t = 48 - t if flip else t
                    total = total + shifted[j, p + i, :, lanes] * taps[t : t + 1, lanes]
            store(p, lanes, total)
        return carry

    lax.fori_loop(first, last, row_step, 0)


def correlate(shifted, grad, out):
    rows, cols, channels = grad.shape
    for h in range(channels // 128):
        lanes = slice(h * 128, (h + 1) * 128)
        for j in range(7):

            def row_step(p, sums):
                own = grad[p, :, lanes].astype(jnp.float32)
                new = []
                for i in range(7):
                    term = shifted[j, p + i, :, lanes] * own
                    new.append(sums[i] + jnp.sum(term.reshape(cols // 8, 8, 128), axis=0))
                return tuple(new)

            sums = lax.fori_loop(
                0, rows, row_step, tuple(jnp.zeros((8, 128), jnp.float32) for _ in range(7))
            )
            for i in range(7):
                out[i * 7 + j : i * 7 + j + 1, lanes] = jnp.sum(sums[i], axis=0, keepdims=True)


def depth_kernel(state, taps, bias, depth_out, pad, shifted, *scratch):
    halo = Halo(state, scratch[:8], *scratch[8:])
    greet_neighbours(0)
    halo.start()
    halo.finish(pad)
    shift_columns(pad, shifted)
    cols = state.shape[1]

    def begin(p, lanes):
        return jnp.broadcast_to(bias[:, lanes], (cols, 128))

    def store(p, lanes, total):
        depth_out[p, :, lanes] = total

    convolve(shifted, taps, begin, 0, state.shape[0], False, store)


def depth_of(state, taps, bias):
    rows, cols, channels = state.shape
    vmem = pl.BlockSpec(memory_space=pltpu.VMEM)
    return pl.pallas_call(
        depth_kernel,
        out_shape=(
            jax.ShapeDtypeStruct(state.shape, jnp.float32),
            jax.ShapeDtypeStruct((rows + 6, cols + 16, channels), jnp.float32),
        ),
        in_specs=[vmem] * 3,
        out_specs=(vmem,) * 2,
        scratch_shapes=[shifted_scratch(rows, cols, channels), *halo_scratch(rows, cols, channels)],
        compiler_params=pltpu.CompilerParams(
            collective_id=1, has_side_effects=True, vmem_limit_bytes=40 * 1024 * 1024
        ),
    )(state, taps, bias[None])


def final_kernel(phases, steps, small_steps, wide_ref, tall_ref, other_ref, grad_ref, pad_ref, cot_ref,
                 taps_ref, wide_out, tall_out, small_out, state_out, *scratch):
    num = len(phases)
    small_mine, mine, whole, small_whole, grad_pad, shifted = scratch[:6]
    scratch = scratch[6:]
    halo = Halo(grad_ref, scratch[:8], *scratch[8:10])
    landing = scratch[10 : 10 + num]
    small_landing = scratch[10 + num : 10 + 2 * num]
    sems = scratch[10 + 2 * num :]
    channels = tall_ref.shape[1]
    depth = wide_ref.shape[0]
    tall = tall_ref.shape[0]
    blocks = wide_ref.shape[1] // channels
    rows = grad_ref.shape[0]
    greet_neighbours(greet(phases))
    halo.start()
    mine[0:tall] = tall_ref[...]
    for b in range(blocks):
        mine[tall + b * depth : tall + (b + 1) * depth] = wide_ref[:, b * channels : (b + 1) * channels]
    big = Reducer(16, steps, mine, whole, landing, *sems[:4])
    small = Reducer(8, small_steps, small_mine, small_whole, small_landing, *sems[4:])

    def small_terms():
        used = 49 + other_ref.shape[0]
        small_mine[49:used] = other_ref[...]
        if used < small_mine.shape[0]:
            small_mine[used:] = jnp.zeros((small_mine.shape[0] - used, channels), jnp.float32)
        shift_columns(pad_ref, shifted)
        correlate(shifted, grad_ref, small_mine)

    def begin(p, lanes):
        return cot_ref[p, :, lanes].astype(jnp.float32)

    def store(p, lanes, total):
        state_out[p, :, lanes] = total.astype(jnp.bfloat16)

    def near_rows():
        halo.finish(grad_pad)
        shift_columns(grad_pad, shifted)
        convolve(shifted, taps_ref, begin, 0, rows // 2, True, store)

    def far_rows():
        convolve(shifted, taps_ref, begin, rows // 2, rows, True, store)

    def chain(reducer):
        moves = []
        for n in range(num):
            moves.append(
                (
                    functools.partial(reducer.scatter_start, n),
                    functools.partial(reducer.scatter_finish, n, n == num - 1),
                )
            )
        for n in reversed(range(num)):
            if reducer.steps[n][3]:
                moves.append(
                    (
                        functools.partial(reducer.gather_start, n),
                        functools.partial(reducer.gather_finish, n),
                    )
                )
        return moves

    lag = 2
    big_moves, small_moves = chain(big), chain(small)
    beside = {1: small_terms, 2: near_rows, 3: far_rows}
    for t in range(max(len(big_moves), len(small_moves) + lag)):
        moves = []
        if 0 <= t - lag < len(small_moves):
            moves.append(small_moves[t - lag])
        if t < len(big_moves):
            moves.append(big_moves[t])
        for start, _ in reversed(moves):
            start()
        if t in beside:
            beside[t]()
        for _, finish in moves:
            finish()
    small_out[...] = small_whole[...]
    tall_out[...] = whole[0:tall]
    for b in range(blocks):
        wide_out[:, b * channels : (b + 1) * channels] = whole[tall + b * depth : tall + (b + 1) * depth]


def final_of(wide, tall, other, grad, pad, cot, taps):
    phases = phases_of(lax.axis_size("lon"), lax.axis_size("lat"))
    num = len(phases)
    channels = tall.shape[1]
    rows = tall.shape[0] + wide.shape[1] // channels * wide.shape[0]
    small_rows = -(-(49 + other.shape[0]) // 64) * 64
    steps, _ = plan(rows, 16, phases)
    small_steps, _ = plan(small_rows, 8, phases)

    def landings(which, dtype):
        return [
            pltpu.VMEM((count, r // count if scatter else r, channels), dtype)
            for axis, stride, count, scatter, r in which
        ]

    vmem = pl.BlockSpec(memory_space=pltpu.VMEM)
    small = (small_rows, channels)
    return pl.pallas_call(
        functools.partial(final_kernel, phases, steps, small_steps),
        out_shape=(
            jax.ShapeDtypeStruct(wide.shape, jnp.bfloat16),
            jax.ShapeDtypeStruct(tall.shape, jnp.bfloat16),
            jax.ShapeDtypeStruct(small, jnp.float32),
            jax.ShapeDtypeStruct(grad.shape, jnp.bfloat16),
        ),
        in_specs=[vmem] * 7,
        out_specs=(vmem,) * 4,
        scratch_shapes=[
            pltpu.VMEM(small, jnp.float32),
            pltpu.VMEM((rows, channels), jnp.bfloat16),
            pltpu.VMEM((rows, channels), jnp.bfloat16),
            pltpu.VMEM(small, jnp.float32),
            pltpu.VMEM(pad.shape, jnp.float32),
            shifted_scratch(*grad.shape),
            *halo_scratch(*grad.shape),
            *landings(steps, jnp.bfloat16),
            *landings(small_steps, jnp.float32),
            *[pltpu.SemaphoreType.DMA((num, 4))] * 8,
        ],
        compiler_params=pltpu.CompilerParams(
            collective_id=0, has_side_effects=True, vmem_limit_bytes=40 * 1024 * 1024
        ),
    )(wide, tall, other, grad, pad, cot, taps)


def forward_tokens(depth_out, ln_gain, ln_bias, w_in, b_in, w_out, b_out):
    center = depth_out - jnp.mean(depth_out, axis=-1, keepdims=True)
    inv_std = lax.rsqrt(jnp.mean(center * center, axis=-1, keepdims=True) + 1e-06)
    norm_hat = center * inv_std
    normed = (norm_hat * ln_gain + ln_bias).astype(jnp.bfloat16)
    pre_act = jnp.dot(normed, w_in, preferred_element_type=jnp.float32) + b_in
    activated = jax.nn.gelu(pre_act, approximate=True).astype(jnp.bfloat16)
    branch = jnp.dot(activated, w_out, preferred_element_type=jnp.float32) + b_out
    return (norm_hat, inv_std, normed, pre_act, activated, branch)


def backward_tokens(masked, norm_hat, inv_std, pre_act, ln_gain, w_in, w_out, layer_scale):
    grad_branch = (masked * layer_scale).astype(jnp.bfloat16)
    grad_act = lax.dot_general(
        grad_branch, w_out, (((1,), (1,)), ((), ())), preferred_element_type=jnp.float32
    )
    unused, pull_back = jax.vjp(lambda v: jax.nn.gelu(v, approximate=True), pre_act)
    grad_pre = pull_back(grad_act)[0].astype(jnp.bfloat16)
    grad_norm = lax.dot_general(
        grad_pre, w_in, (((1,), (1,)), ((), ())), preferred_element_type=jnp.float32
    )
    scaled = grad_norm * ln_gain
    grad_depth = (
        inv_std
        * (
            scaled
            - jnp.mean(scaled, axis=-1, keepdims=True)
            - norm_hat * jnp.mean(scaled * norm_hat, axis=-1, keepdims=True)
        )
    ).astype(jnp.bfloat16)
    return (grad_branch, grad_pre, grad_norm, grad_depth)


def weight_terms(masked, branch, grad_branch, activated, normed, grad_pre, grad_norm, norm_hat):
    dims = (((0,), (0,)), ((), ()))
    grad_w_in = lax.dot_general(normed, grad_pre, dims, preferred_element_type=jnp.float32)
    grad_w_out = lax.dot_general(activated, grad_branch, dims, preferred_element_type=jnp.float32)
    return (
        grad_w_in,
        grad_w_out,
        jnp.sum(grad_pre.astype(jnp.float32), axis=0),
        jnp.sum(grad_branch.astype(jnp.float32), axis=0),
        jnp.sum(masked * branch, axis=0),
        jnp.sum(grad_norm * norm_hat, axis=0),
        jnp.sum(grad_norm, axis=0),
    )


def local(
    ocean_state,
    land_sea,
    cotangent,
    dw_kernel,
    dw_bias,
    ln_gain,
    ln_bias,
    w_in,
    b_in,
    w_out,
    b_out,
    layer_scale,
):
    num_batch, num_rows, num_cols, channels = ocean_state.shape
    mask_float = land_sea.astype(jnp.float32)[..., None]
    taps = dw_kernel.reshape(-1, channels)
    depth_out, padded = depth_of(ocean_state[0], taps, dw_bias)
    masked = (mask_float * cotangent.astype(jnp.float32)).reshape(-1, channels)
    norm_hat, inv_std, normed, pre_act, activated, branch = forward_tokens(
        depth_out.reshape(-1, channels), ln_gain, ln_bias, w_in, b_in, w_out, b_out
    )
    grad_branch, grad_pre, grad_norm, grad_flat = backward_tokens(
        masked, norm_hat, inv_std, pre_act, ln_gain, w_in, w_out, layer_scale
    )
    grad_terms = weight_terms(
        masked, branch, grad_branch, activated, normed, grad_pre, grad_norm, norm_hat
    )
    grad_depth = grad_flat.reshape(num_batch, num_rows, num_cols, channels)
    branch_own = branch.reshape(num_batch, num_rows, num_cols, channels)
    output = (ocean_state.astype(jnp.float32) + mask_float * layer_scale * branch_own).astype(
        jnp.bfloat16
    )
    bias_part = jnp.sum(grad_depth.astype(jnp.float32), axis=(0, 1, 2))
    grad_w_in, grad_w_out, grad_b_in, grad_b_out, grad_scale, grad_ln_gain, grad_ln_bias = (
        grad_terms
    )
    rows = [
        bias_part[None],
        grad_ln_gain[None],
        grad_ln_bias[None],
        grad_b_out[None],
        grad_scale[None],
        grad_b_in.reshape(-1, channels),
    ]
    grad_w_in, grad_w_out, small, grad_state = final_of(
        grad_w_in.astype(jnp.bfloat16),
        grad_w_out.astype(jnp.bfloat16),
        jnp.concatenate(rows),
        grad_depth[0],
        padded,
        cotangent[0],
        taps,
    )
    grad_state = grad_state[None]
    grad_w_in, grad_w_out = (grad_w_in.astype(jnp.float32), grad_w_out.astype(jnp.float32))
    all_cells = num_batch * num_rows * num_cols * lax.axis_size("lon") * lax.axis_size("lat")
    factor = 1.0 / jnp.sqrt(jnp.float32(all_cells))
    small = small * factor
    return (
        output,
        grad_state,
        small[:49].reshape(7, 7, channels),
        small[49],
        small[50],
        small[51],
        grad_w_in * factor,
        small[54 : 54 + b_in.shape[0] // channels].reshape(-1),
        grad_w_out * factor,
        small[52],
        small[53],
    )


def solution(mesh):
    in_specs = (
        P(None, "lat", "lon", None),
        P(None, "lat", "lon"),
        P(None, "lat", "lon", None),
        P(),
        P(),
        P(),
        P(),
        P(),
        P(),
        P(),
        P(),
        P(),
    )
    out_specs = (
        P(None, "lat", "lon", None),
        P(None, "lat", "lon", None),
        P(),
        P(),
        P(),
        P(),
        P(),
        P(),
        P(),
        P(),
        P(),
    )
    return jax.shard_map(local, mesh=mesh, in_specs=in_specs, out_specs=out_specs, check_vma=False)
```
